32 devices in a mesh: grp: 2 (over x), ctx: 16 (over z, y, core).
Axes of the slice: x: 2, y: 2, z: 4, core: 2. Of those that a mesh axis runs over, the one named last changes fastest.
Arguments:
- query_proj: bfloat16 [4096, 4096], P(('grp', 'ctx')), parts along dimension 0, may hold values from -6 to 6
- key_proj: bfloat16 [4096, 4096], P(('grp', 'ctx')), parts along dimension 0, may hold values from -6 to 6
- value_proj: bfloat16 [4096, 4096], P(('grp', 'ctx')), parts along dimension 0, may hold values from -6 to 6
- out_grad: bfloat16 [4096, 4096], P(('grp', 'ctx')), parts along dimension 0, may hold values from -18 to 18
- short_taps: bfloat16 [7, 12288], replicated, may hold values from -2.5 to 2.5
- medium_taps: bfloat16 [256, 128], replicated, may hold values from -6 to 6
- doc_starts: int32 [32, 2], P(('grp', 'ctx')), parts along dimension 0, may hold values from 0 to 1023
- continues: int32 [32], P(('grp', 'ctx')), parts along dimension 0, may hold values 0 or 1
Outputs:
- gated: bfloat16 [4096, 4096], P(('grp', 'ctx')), parts along dimension 0
- grad_query: bfloat16 [4096, 4096], P(('grp', 'ctx')), parts along dimension 0
- grad_key: bfloat16 [4096, 4096], P(('grp', 'ctx')), parts along dimension 0
- grad_value: bfloat16 [4096, 4096], P(('grp', 'ctx')), parts along dimension 0
- grad_short: float32 [14, 12288], P('grp'), parts along dimension 0
- grad_medium: float32 [512, 128], P('grp'), parts along dimension 0
The draws below stay inside these ranges and needn't reach their ends.
There are 2 independent parts, one for each index of `grp`. The reference program is written for one: setup_inputs(seed, part) draws one part's arguments, and reference() takes and returns one part's arrays. A program takes and returns all parts, laid end to end along the dimension named above; an argument that names none is the same for every part. Nothing has to cross between parts.
Inputs may be any that keep to these rules, and one draw needn't show every extreme that they name: `doc_starts`: an entry below 128 is the offset of a document start in that block; larger entries mark no start.
All inputs are finite; a program needn't handle non-finite values. No bound on the sum of `continues` on one device may be relied on, other than what follows from the above.
Results may differ from the reference program's by a relative error of at most 0.0059.
Values may be sent and summed in bfloat16 or wider, within the bound.
A program may use at most 192 MiB of HBM per device.

```python
import math
import jax
import jax.numpy as jnp
from jax import lax

CHANNELS = 4096
GROUP_SIZE = 16
FIR_LEN = 7
MED_LEN = 128
DOCUMENT_SLOTS = 2
T_DEV = 128
GROUPS = 256
TOKENS = 2048
N_CTX = 16


def draw_medium_taps(key, part):
    key = jax.random.fold_in(key, 11)
    keys = jax.random.split(key, 3)
    rates = jnp.exp(jax.random.uniform(keys[0], (GROUPS, 1), jnp.float32, jnp.log(0.003), jnp.log(0.03)))
    gaussian_jitter = jnp.clip(jax.random.normal(keys[1], (GROUPS, MED_LEN), jnp.float32), -6.0, 6.0)
    sequence_indices = jnp.arange(MED_LEN, dtype=jnp.int32)
    boundary_cuts = jax.random.randint(keys[2], (GROUPS, 3), 1, MED_LEN)
    spike_shape = jnp.prod(jnp.where(sequence_indices[None, :, None] >= boundary_cuts[:, None, :], 0.6, 1.0), axis=2)
    damping_ratio = jnp.exp(-rates * sequence_indices[None, :].astype(jnp.float32))
    magnitude_scalar = jnp.sqrt((1.0 - jnp.exp(-2.0 * rates * MED_LEN)) / (1.0 - jnp.exp(-2.0 * rates)))
    return (gaussian_jitter * damping_ratio * spike_shape / magnitude_scalar).astype(jnp.bfloat16)


def draw_out_grad(key, part):
    key = jax.random.fold_in(key, 23)
    keys = jax.random.split(key, 2)
    rising = jnp.exp(jnp.log(3.0) * jnp.arange(TOKENS, dtype=jnp.float32) / TOKENS)[:, None]
    gaussian_jitter = jnp.clip(jax.random.normal(keys[1], (TOKENS, CHANNELS), jnp.float32), -6.0, 6.0)
    return (gaussian_jitter * rising).astype(jnp.bfloat16)


def plant(result, stream_key, low, largest):
    longest = result.shape.index(max(result.shape))
    spots = []
    for shift in (0, 1):
        where = [jax.random.randint(jax.random.fold_in(stream_key, axis), (), 0, length) for axis, length in enumerate(result.shape)]
        where[longest] = (where[longest] + shift) % result.shape[longest]
        spots.append(tuple(where))
    return result.at[spots[0]].set(low).at[spots[1]].set(largest)


def shard_levels(stream_key, extent, shards, least, high):
    gain, own = 1.0, jax.random.fold_in(stream_key, 6)
    for dim, shards_of in shards:
        heights = jnp.exp(jax.random.uniform(jax.random.fold_in(own, dim), (shards_of,), jnp.float32, least / len(shards), high / len(shards)))
        gain = gain * jnp.repeat(heights, extent[dim] // shards_of).reshape([-1 if axis == dim else 1 for axis in range(len(extent))])
    return gain


def scatter_about(rng, dims, deviation, limit, shards=(), held_as=jnp.bfloat16):
    factor_of = shard_levels(rng, dims, shards, -0.22, 0.18) if shards else 1.0
    entries = jax.random.normal(rng, dims, jnp.float32) * deviation * factor_of
    return jnp.minimum(jnp.maximum(entries, -limit), limit).astype(held_as)


def setup_inputs(seed: int = 0, part: int = 0) -> dict:
    seeds = jax.random.split(jax.random.key(seed), 9)
    own_keys = jax.random.split(jax.random.fold_in(seeds[8], part), 9)
    query_proj = scatter_about(own_keys[0], (TOKENS, CHANNELS), 1.0, 6.0, ((0, 16),))
    key_proj = scatter_about(own_keys[1], (TOKENS, CHANNELS), 1.0, 6.0, ((0, 16),))
    value_proj = scatter_about(own_keys[2], (TOKENS, CHANNELS), 1.0, 6.0, ((0, 16),))
    out_grad = draw_out_grad(jax.random.fold_in(jax.random.fold_in(seeds[8], part), 71), part)
    short_taps = scatter_about(seeds[4], (FIR_LEN, 3 * CHANNELS), 0.4, 2.5)
    medium_taps = draw_medium_taps(jax.random.fold_in(seeds[8], 71), part)
    doc_starts = plant(jax.random.randint(own_keys[6], (N_CTX, DOCUMENT_SLOTS), 0, 8 * T_DEV), jax.random.fold_in(own_keys[6], 1), 0, (8 * T_DEV) - 1).astype(jnp.int32)
    continues = plant((jax.random.randint(own_keys[7], (N_CTX,), 0, 4) < 3).astype(jnp.int32), jax.random.fold_in(own_keys[7], 1), 0, 1)
    return {"query_proj": query_proj, "key_proj": key_proj, "value_proj": value_proj, "out_grad": out_grad, "short_taps": short_taps, "medium_taps": medium_taps, "doc_starts": doc_starts, "continues": continues}


def segment_ids(doc_starts, continues):
    position = jnp.arange(TOKENS, dtype=jnp.int32)
    shard_index = position // T_DEV
    offset = position - shard_index * T_DEV
    listed = jnp.any(doc_starts[shard_index] == offset[:, None], axis=1)
    opened = listed | (offset == 0) & (continues[shard_index] == 0)
    return jnp.cumsum(opened.astype(jnp.int32)).astype(jnp.int32)

def earlier(values, delay, filler):
    front = jnp.full((delay,) + values.shape[1:], filler, values.dtype)
    return jnp.concatenate([front, values[:values.shape[0] - delay]], axis=0)

def later(values, delay, filler):
    back = jnp.full((delay,) + values.shape[1:], filler, values.dtype)
    return jnp.concatenate([values[delay:], back], axis=0)

def short_forward(signal, taps, segment):
    running = jnp.zeros(signal.shape, jnp.float32)
    for delay in range(FIR_LEN):
        same_doc = (earlier(segment, delay, -1) == segment).astype(jnp.float32)[:, None]
        running = running + taps[delay][None, :] * earlier(signal, delay, 0.0) * same_doc
    return running

def short_backward(grads, taps, segment):
    running = jnp.zeros(grads.shape, jnp.float32)
    for delay in range(FIR_LEN):
        same_doc = (later(segment, delay, -1) == segment).astype(jnp.float32)[:, None]
        running = running + taps[delay][None, :] * later(grads, delay, 0.0) * same_doc
    return running

def short_taps_grad(grads, signal, segment):
    rows_out = []
    for delay in range(FIR_LEN):
        same_doc = (earlier(segment, delay, -1) == segment).astype(jnp.float32)[:, None]
        rows_out.append(lax.optimization_barrier(jnp.sum(grads * earlier(signal, delay, 0.0) * same_doc, axis=0)))
    return jnp.stack(rows_out)

def long_forward(mixed, taps, segment):
    channels = mixed.shape[1]
    padded = jnp.concatenate([jnp.zeros((MED_LEN, channels), jnp.float32), mixed], axis=0)
    labels = jnp.concatenate([jnp.full((MED_LEN,), -1, jnp.int32), segment], axis=0)

    def advance(tap_index, running):
        first_row = (MED_LEN - tap_index).astype(jnp.int32)
        shifted = lax.dynamic_slice_in_dim(padded, first_row, TOKENS, 0)
        shifted_labels = lax.dynamic_slice_in_dim(labels, first_row, TOKENS, 0)
        same_doc = (shifted_labels == segment).astype(jnp.float32)[:, None]
        weight = lax.dynamic_index_in_dim(taps, tap_index, 0, keepdims=False)
        return running + weight[None, :] * shifted * same_doc
    return lax.fori_loop(jnp.int32(0), jnp.int32(MED_LEN), advance, jnp.zeros((TOKENS, channels), jnp.float32))

def long_backward(grads, taps, segment):
    channels = grads.shape[1]
    padded = jnp.concatenate([grads, jnp.zeros((MED_LEN, channels), jnp.float32)], axis=0)
    labels = jnp.concatenate([segment, jnp.full((MED_LEN,), -1, jnp.int32)], axis=0)

    def advance(tap_index, running):
        first_row = tap_index.astype(jnp.int32)
        shifted = lax.dynamic_slice_in_dim(padded, first_row, TOKENS, 0)
        shifted_labels = lax.dynamic_slice_in_dim(labels, first_row, TOKENS, 0)
        same_doc = (shifted_labels == segment).astype(jnp.float32)[:, None]
        weight = lax.dynamic_index_in_dim(taps, tap_index, 0, keepdims=False)
        return running + weight[None, :] * shifted * same_doc
    return lax.fori_loop(jnp.int32(0), jnp.int32(MED_LEN), advance, jnp.zeros((TOKENS, channels), jnp.float32))

def long_taps_grad(grads, mixed, segment):
    channels = mixed.shape[1]
    padded = jnp.concatenate([jnp.zeros((MED_LEN, channels), jnp.float32), mixed], axis=0)
    labels = jnp.concatenate([jnp.full((MED_LEN,), -1, jnp.int32), segment], axis=0)

    def advance(tap_index, running):
        first_row = (MED_LEN - tap_index).astype(jnp.int32)
        shifted = lax.dynamic_slice_in_dim(padded, first_row, TOKENS, 0)
        shifted_labels = lax.dynamic_slice_in_dim(labels, first_row, TOKENS, 0)
        same_doc = (shifted_labels == segment).astype(jnp.float32)[:, None]
        summed = lax.optimization_barrier(jnp.sum(grads * shifted * same_doc, axis=0))
        return lax.dynamic_update_index_in_dim(running, summed, tap_index, 0)
    return lax.fori_loop(jnp.int32(0), jnp.int32(MED_LEN), advance, jnp.zeros((MED_LEN, channels), jnp.float32))

def reference(query_proj, key_proj, value_proj, out_grad, short_taps, medium_taps, doc_starts, continues):
    segment = segment_ids(doc_starts, continues)
    block_width = math.gcd(CHANNELS, 128)
    block_count = CHANNELS // block_width

    def blocked(values):
        return values.reshape(values.shape[0], block_count, block_width).transpose(1, 0, 2)
    taps_f = short_taps.astype(jnp.float32)
    per_channel = jnp.repeat(medium_taps.astype(jnp.float32), GROUP_SIZE, axis=0).T
    pieces = (blocked(query_proj), blocked(key_proj), blocked(value_proj), blocked(out_grad), blocked(taps_f[:, :CHANNELS]), blocked(taps_f[:, CHANNELS:2 * CHANNELS]), blocked(taps_f[:, 2 * CHANNELS:]), blocked(per_channel))

    def one_piece(piece):
        query_b, key_b, value_b, grad_b, taps_q, taps_k, taps_v, long_filter_taps = piece
        query_x = query_b.astype(jnp.float32)
        key_x = key_b.astype(jnp.float32)
        value_x = value_b.astype(jnp.float32)
        grad_x = grad_b.astype(jnp.float32)
        query_f = short_forward(query_x, taps_q, segment)
        key_f = short_forward(key_x, taps_k, segment)
        value_f = short_forward(value_x, taps_v, segment)
        mixed = (key_f * value_f).astype(jnp.bfloat16).astype(jnp.float32)
        long_conv = long_forward(mixed, long_filter_taps, segment)
        gated = (query_f * long_conv).astype(jnp.bfloat16)
        conv_grad = (grad_x * query_f).astype(jnp.bfloat16).astype(jnp.float32)
        mixed_grad = long_backward(conv_grad, long_filter_taps, segment)
        grad_qf = (grad_x * long_conv).astype(jnp.bfloat16).astype(jnp.float32)
        grad_kf = (mixed_grad * value_f).astype(jnp.bfloat16).astype(jnp.float32)
        grad_vf = (mixed_grad * key_f).astype(jnp.bfloat16).astype(jnp.float32)
        grad_q = short_backward(grad_qf, taps_q, segment).astype(jnp.bfloat16)
        grad_k = short_backward(grad_kf, taps_k, segment).astype(jnp.bfloat16)
        grad_v = short_backward(grad_vf, taps_v, segment).astype(jnp.bfloat16)
        short_q = short_taps_grad(grad_qf, query_x, segment)
        short_k = short_taps_grad(grad_kf, key_x, segment)
        short_v = short_taps_grad(grad_vf, value_x, segment)
        long_grad = long_taps_grad(conv_grad, mixed, segment)
        long_grad = long_grad.reshape(MED_LEN, block_width // GROUP_SIZE, GROUP_SIZE).sum(axis=2)
        return (gated, grad_q, grad_k, grad_v, short_q, short_k, short_v, long_grad)
    results = lax.map(one_piece, pieces)

    def tokens_back(values):
        return values.transpose(1, 0, 2).reshape(TOKENS, CHANNELS)

    def taps_back(values):
        return values.transpose(1, 0, 2).reshape(FIR_LEN, CHANNELS)
    grad_short = jnp.concatenate([taps_back(results[4]), taps_back(results[5]), taps_back(results[6])], axis=1)
    grad_short = grad_short / math.sqrt(TOKENS)
    grad_medium = results[7].transpose(0, 2, 1).reshape(GROUPS, MED_LEN) / math.sqrt(TOKENS * GROUP_SIZE)
    return (tokens_back(results[0]), tokens_back(results[1]), tokens_back(results[2]), tokens_back(results[3]), grad_short, grad_medium)
```

```python
import functools
import math

import jax
import jax.numpy as jnp
from jax import lax
from jax.experimental import pallas as pl
from jax.experimental.pallas import tpu as pltpu
from jax.sharding import PartitionSpec as P

LANES = 128
HALO = 8
WIDE = 512
VMEM_BYTES = 48 * 1024 * 1024
F32 = jnp.float32
BF16 = jnp.bfloat16


def labels(position, starts, flag, length):
    position = jnp.minimum(position, length - 1)
    label = (flag[0] == 0).astype(jnp.int32)
    label = label + (starts[0, 0] <= position).astype(jnp.int32)
    label = label + (starts[0, 1] <= position).astype(jnp.int32)
    return jnp.where(position < 0, 0, label)


def short_forward(
    starts, flag, q_ref, k_ref, v_ref, og_ref, hq_ref, hk_ref, hv_ref, wq_ref, wk_ref, wv_ref,
    mixed_ref, grad_ref, mixed_out_ref, grad_out_ref, qf_ref, kf_ref, vf_ref, masks, ext,
):
    length = q_ref.shape[0]
    taps = wq_ref.shape[0]
    row = lax.broadcasted_iota(jnp.int32, (length, LANES), 0)

    @pl.when(pl.program_id(0) == 0)
    def _():
        own = labels(row, starts, flag, length)
        last = labels(row * 0 + (length - 1), starts, flag, length)
        for j in range(taps):
            masks[j] = (labels(row - j, starts, flag, length) == own).astype(F32)
        masks[taps] = (own == last).astype(F32)
        masks[taps + 1] = (own == 0).astype(F32)

    def tile(i, carry):
        cols = pl.ds(pl.multiple_of(i * LANES, LANES), LANES)
        filtered = []
        for n, (x, h, w, out) in enumerate(
            ((q_ref, hq_ref, wq_ref, qf_ref), (k_ref, hk_ref, wk_ref, kf_ref), (v_ref, hv_ref, wv_ref, vf_ref))
        ):
            ext[n, :HALO, :] = h[:, cols]
            ext[n, HALO:, :] = x[:, cols].astype(F32)
            weight = w[:, cols]
            total = weight[0:1] * ext[n, HALO:, :]
            for j in range(1, taps):
                total = total + weight[j : j + 1] * (ext[n, HALO - j : HALO - j + length, :] * masks[j])
            out[:, cols] = total
            filtered.append(total)
        query, key, value = filtered
        mixed = (key * value).astype(BF16)
        mixed_ref[:, cols] = mixed
        mixed_out_ref[:, cols] = (mixed.astype(F32) * masks[taps]).astype(BF16)
        grad = (og_ref[:, cols].astype(F32) * query).astype(BF16)
        grad_ref[:, cols] = grad
        grad_out_ref[:, cols] = (grad.astype(F32) * masks[taps + 1]).astype(BF16)
        return carry

    lax.fori_loop(0, q_ref.shape[1] // LANES, tile, 0)


def long_filter(
    starts, flag, mixed_ref, before_ref, grad_ref, after_ref, qf_ref, kf_ref, vf_ref, og_ref,
    taps_ref, turned_ref, gated_ref, sq_ref, sk_ref, sv_ref, dmed_ref,
    masks, rev_masks, back, left, left_t, left_p, prod, prod_t, prod_p,
):
    length = mixed_ref.shape[0]
    size = mixed_ref.shape[1] // taps_ref.shape[0]
    per_tile = LANES // size
    row = lax.broadcasted_iota(jnp.int32, (length, length), 0)
    col = lax.broadcasted_iota(jnp.int32, (length, length), 1)

    @pl.when(pl.program_id(0) == 0)
    def _():
        label_row = labels(row, starts, flag, length)
        label_col = labels(col, starts, flag, length)
        last = labels(row * 0 + (length - 1), starts, flag, length)
        same = label_row == label_col
        masks[0] = ((col <= row) & same).astype(F32).astype(BF16)
        masks[1] = ((col > row) & (label_row == 0)).astype(F32).astype(BF16)
        masks[2] = ((col >= row) & same).astype(F32).astype(BF16)
        masks[3] = ((col < row) & (label_row == last)).astype(F32).astype(BF16)
        rev = (length - 1) - row
        label_rev = labels(rev, starts, flag, length)
        rev_masks[0] = ((col <= rev) & (label_rev == label_col)).astype(F32)
        rev_masks[1] = ((col > rev) & (label_rev == 0)).astype(F32)
        back[...] = (row + col == length - 1).astype(F32).astype(BF16)

    group_of_lane = lax.broadcasted_iota(jnp.int32, (length, LANES), 1) // size

    def tile(i, carry):
        cols = pl.ds(pl.multiple_of(i * LANES, LANES), LANES)
        rows = pl.ds(pl.multiple_of(i * per_tile, per_tile), per_tile)
        taps = taps_ref[rows, :]
        turned = turned_ref[rows, :]
        mixed = mixed_ref[:, cols]
        grad = grad_ref[:, cols]
        both = jnp.concatenate([mixed, before_ref[:, cols]], axis=0)
        both_grad = jnp.concatenate([grad, after_ref[:, cols]], axis=0)
        flipped = jnp.dot(back[...], grad, preferred_element_type=F32)
        for g in range(per_tile):
            part = slice(g * length, (g + 1) * length)
            ring = pltpu.roll(
                jnp.broadcast_to(turned[g : g + 1], (length, length)), 0, 1, stride=1, stride_axis=0
            ).astype(BF16)
            left[part, :length] = ring * masks[0]
            left[part, length:] = ring * masks[1]
            ring_t = pltpu.roll(
                jnp.broadcast_to(taps[g : g + 1], (length, length)), 0, 1, stride=1, stride_axis=0
            ).astype(BF16)
            left_t[part, :length] = ring_t * masks[2]
            left_t[part, length:] = ring_t * masks[3]
            left_p[part, :] = jnp.where(group_of_lane == g, flipped, 0.0).astype(BF16)
        prod[...] = jnp.dot(left[...], both, preferred_element_type=F32)
        prod_t[...] = jnp.dot(left_t[...], both_grad, preferred_element_type=F32)
        prod_p[...] = lax.dot_general(
            left_p[...], both, (((1,), (1,)), ((), ())), preferred_element_type=F32
        )
        conv = prod[:length, :]
        mixed_grad = prod_t[:length, :]
        sums = []
        for g in range(per_tile):
            part = slice(g * length, (g + 1) * length)
            if g:
                conv = jnp.where(group_of_lane == g, prod[part, :], conv)
                mixed_grad = jnp.where(group_of_lane == g, prod_t[part, :], mixed_grad)
            pair = prod_p[part, :length] * rev_masks[0] + prod_p[part, length:] * rev_masks[1]
            pair = pltpu.roll(pair, 0, 1, stride=1, stride_axis=0)
            sums.append(jnp.sum(pair, axis=0, keepdims=True))
        dmed_ref[rows, :] = jnp.concatenate(sums, axis=0)
        gated_ref[:, cols] = (qf_ref[:, cols] * conv).astype(BF16)
        sq_ref[:, cols] = (og_ref[:, cols].astype(F32) * conv).astype(BF16)
        sk_ref[:, cols] = (mixed_grad * vf_ref[:, cols]).astype(BF16)
        sv_ref[:, cols] = (mixed_grad * kf_ref[:, cols]).astype(BF16)
        return carry

    lax.fori_loop(0, mixed_ref.shape[1] // LANES, tile, 0)


def short_backward(
    starts, flag, sq_ref, sk_ref, sv_ref, hq_ref, hk_ref, hv_ref, q_ref, k_ref, v_ref, wq_ref, wk_ref, wv_ref,
    gq_ref, gk_ref, gv_ref, dq_ref, dk_ref, dv_ref, masks, ext,
):
    length = q_ref.shape[0]
    taps = wq_ref.shape[0]
    row = lax.broadcasted_iota(jnp.int32, (length, LANES), 0)

    @pl.when(pl.program_id(0) == 0)
    def _():
        own = labels(row, starts, flag, length)
        for j in range(taps):
            masks[j] = (labels(row + j, starts, flag, length) == own).astype(F32)

    def tile(i, carry):
        cols = pl.ds(pl.multiple_of(i * LANES, LANES), LANES)
        for n, (s, h, x, w, out, d) in enumerate((
            (sq_ref, hq_ref, q_ref, wq_ref, gq_ref, dq_ref),
            (sk_ref, hk_ref, k_ref, wk_ref, gk_ref, dk_ref),
            (sv_ref, hv_ref, v_ref, wv_ref, gv_ref, dv_ref),
        )):
            ext[n, :length, :] = s[:, cols].astype(F32)
            ext[n, length:, :] = h[:, cols]
            weight = w[:, cols]
            signal = x[:, cols].astype(F32)
            total = jnp.zeros((length, LANES), F32)
            sums = []
            for j in range(taps):
                moved = ext[n, j : j + length, :]
                if j:
                    moved = moved * masks[j]
                total = total + weight[j : j + 1] * moved
                sums.append(jnp.sum(signal * moved, axis=0, keepdims=True))
            sums.append(jnp.zeros((HALO - taps, LANES), F32))
            out[:, cols] = total.astype(BF16)
            d[:, cols] = jnp.concatenate(sums, axis=0)
        return carry

    lax.fori_loop(0, q_ref.shape[1] // LANES, tile, 0)


def all_sum(count, short_scale, med_scale, short_ref, med_ref, short_out, med_out, short_in, med_in, send, recv):
    me = lax.axis_index("ctx")
    columns = short_ref.shape[1] // count
    rows = med_ref.shape[0] // count

    def cols_of(peer):
        return pl.ds(pl.multiple_of(peer * columns, columns), columns)

    def rows_of(peer):
        return pl.ds(pl.multiple_of(peer * rows, rows), rows)

    barrier = pltpu.get_barrier_semaphore()
    for d in range(1, count):
        pl.semaphore_signal(
            barrier, inc=1, device_id={"ctx": lax.rem(me + d, count)}, device_id_type=pl.DeviceIdType.MESH
        )
    pl.semaphore_wait(barrier, count - 1)

    def copy(src, dst, phase, d):
        return pltpu.make_async_remote_copy(
            src_ref=src, dst_ref=dst, send_sem=send.at[phase, d], recv_sem=recv.at[phase, d],
            device_id={"ctx": lax.rem(me + d, count)}, device_id_type=pl.DeviceIdType.MESH,
        )

    first = []
    for d in range(1, count):
        peer = lax.rem(me + d, count)
        first.append(copy(short_ref.at[:, cols_of(peer)], short_in.at[d], 0, d))
        first.append(copy(med_ref.at[rows_of(peer), :], med_in.at[d], 1, d))
    for c in first:
        c.start()
    short_total = short_ref[:, cols_of(me)]
    med_total = med_ref[rows_of(me), :]
    for c in first:
        c.wait_recv()
    for d in range(1, count):
        short_total = short_total + short_in[d]
        med_total = med_total + med_in[d]
    short_out[:, cols_of(me)] = short_total * short_scale
    med_out[rows_of(me), :] = med_total * med_scale
    second = []
    for d in range(1, count):
        mine = short_out.at[:, cols_of(me)]
        second.append(copy(mine, mine, 2, d))
        mine = med_out.at[rows_of(me), :]
        second.append(copy(mine, mine, 3, d))
    for c in second:
        c.start()
    for c in second:
        c.wait_recv()
    for c in first + second:
        c.wait_send()


def params(**kwargs):
    return pltpu.CompilerParams(vmem_limit_bytes=VMEM_BYTES, **kwargs)


def local(query_proj, key_proj, value_proj, out_grad, short_taps, medium_taps, doc_starts, continues):
    length, channels = query_proj.shape
    groups, med_len = medium_taps.shape
    size = channels // groups
    fir_len = short_taps.shape[0]
    reach = fir_len - 1
    peers = lax.axis_size("ctx")
    up = [(i, i + 1) for i in range(peers - 1)]
    down = [(i + 1, i) for i in range(peers - 1)]

    position = jnp.arange(length, dtype=jnp.int32)
    segment = labels(position, doc_starts, continues, length)
    closing = (segment == segment[length - 1]).astype(F32)[:, None]
    opening = (segment == 0).astype(F32)[:, None]

    tails = jnp.concatenate([x[length - reach :] for x in (query_proj, key_proj, value_proj)], axis=1)
    tails = (tails.astype(F32) * closing[length - reach :]).astype(BF16)
    before = jnp.pad(lax.ppermute(tails, "ctx", up).astype(F32), ((HALO - reach, 0), (0, 0)))
    taps_f = short_taps.astype(F32)
    steps = channels // WIDE
    smem = [pl.BlockSpec(memory_space=pltpu.SMEM)] * 2

    def wide(rows, part=0):
        return pl.BlockSpec((rows, WIDE), lambda i: (0, i + part * steps))

    shape = jax.ShapeDtypeStruct
    half = shape((length, channels), BF16)
    full = shape((length, channels), F32)
    parts = [0, 1, 2]
    mixed, grad, mixed_out, grad_out, qf, kf, vf = pl.pallas_call(
        short_forward,
        grid=(steps,),
        in_specs=smem + [wide(length)] * 4 + [wide(HALO, p) for p in parts] + [wide(fir_len, p) for p in parts],
        out_specs=[wide(length)] * 7,
        out_shape=[half] * 4 + [full] * 3,
        scratch_shapes=[
            pltpu.VMEM((fir_len + 2, length, LANES), F32),
            pltpu.VMEM((3, HALO + length, LANES), F32),
        ],
        compiler_params=params(),
    )(doc_starts, continues, query_proj, key_proj, value_proj, out_grad, before, before, before, taps_f, taps_f, taps_f)

    mixed_before = lax.ppermute(mixed_out, "ctx", up)
    grad_after = lax.ppermute(grad_out, "ctx", down)

    med_f = medium_taps.astype(F32)
    turned = jnp.roll(jnp.flip(med_f, axis=1), 1, axis=1)
    per_tile = LANES // size
    med_spec = pl.BlockSpec((WIDE // size, med_len), lambda i: (i, 0))
    gated, sq, sk, sv, dmed = pl.pallas_call(
        long_filter,
        grid=(steps,),
        in_specs=smem + [wide(length)] * 8 + [med_spec] * 2,
        out_specs=[wide(length)] * 4 + [med_spec],
        out_shape=[half] * 4 + [shape((groups, med_len), F32)],
        scratch_shapes=[
            pltpu.VMEM((4, length, length), BF16),
            pltpu.VMEM((2, length, length), F32),
            pltpu.VMEM((length, length), BF16),
            pltpu.VMEM((per_tile * length, 2 * length), BF16),
            pltpu.VMEM((per_tile * length, 2 * length), BF16),
            pltpu.VMEM((per_tile * length, LANES), BF16),
            pltpu.VMEM((per_tile * length, LANES), F32),
            pltpu.VMEM((per_tile * length, LANES), F32),
            pltpu.VMEM((per_tile * length, 2 * length), F32),
        ],
        compiler_params=params(),
    )(doc_starts, continues, mixed, mixed_before, grad, grad_after, qf, kf, vf, out_grad, med_f, turned)

    heads = jnp.concatenate([s[:reach] for s in (sq, sk, sv)], axis=1)
    heads = (heads.astype(F32) * opening[:reach]).astype(BF16)
    after = jnp.pad(lax.ppermute(heads, "ctx", down).astype(F32), ((0, HALO - reach), (0, 0)))
    eight = shape((HALO, channels), F32)
    gq, gk, gv, dq, dk, dv = pl.pallas_call(
        short_backward,
        grid=(steps,),
        in_specs=smem
        + [wide(length)] * 3
        + [wide(HALO, p) for p in parts]
        + [wide(length)] * 3
        + [wide(fir_len, p) for p in parts],
        out_specs=[wide(length)] * 3 + [wide(HALO)] * 3,
        out_shape=[half] * 3 + [eight] * 3,
        scratch_shapes=[
            pltpu.VMEM((fir_len, length, LANES), F32),
            pltpu.VMEM((3, length + HALO, LANES), F32),
        ],
        compiler_params=params(),
    )(doc_starts, continues, sq, sk, sv, after, after, after, query_proj, key_proj, value_proj, taps_f, taps_f, taps_f)

    dshort = jnp.concatenate([dq, dk, dv], axis=1)
    tokens = length * peers
    short_scale = 1.0 / math.sqrt(tokens)
    med_scale = 1.0 / math.sqrt(tokens * size)
    if (3 * channels) % (peers * LANES) == 0 and groups % (peers * 8) == 0:
        columns, rows = 3 * channels // peers, groups // peers
        dshort, dmed = pl.pallas_call(
            functools.partial(all_sum, peers, short_scale, med_scale),
            in_specs=[pl.BlockSpec(memory_space=pltpu.VMEM)] * 2,
            out_specs=[pl.BlockSpec(memory_space=pltpu.VMEM)] * 2,
            out_shape=[shape(dshort.shape, F32), shape(dmed.shape, F32)],
            scratch_shapes=[
                pltpu.VMEM((peers, HALO, columns), F32),
                pltpu.VMEM((peers, rows, med_len), F32),
                pltpu.SemaphoreType.DMA((4, peers)),
                pltpu.SemaphoreType.DMA((4, peers)),
            ],
            compiler_params=params(collective_id=0, has_side_effects=True),
        )(dshort, dmed)
    else:
        dshort, dmed = lax.psum((dshort, dmed), "ctx")
        dshort, dmed = dshort * short_scale, dmed * med_scale
    return gated, gq, gk, gv, dshort[:fir_len], jnp.flip(dmed, axis=1)


def solution(mesh):
    tokens = P(("grp", "ctx"), None)
    in_specs = (tokens,) * 4 + (P(), P(), tokens, P(("grp", "ctx")))
    out_specs = (tokens,) * 4 + (P("grp", None), P("grp", None))
    return jax.shard_map(local, mesh=mesh, in_specs=in_specs, out_specs=out_specs, check_vma=False)
```

```python
import functools
import math

import jax
import jax.numpy as jnp
from jax import lax
from jax.experimental import pallas as pl
from jax.experimental.pallas import tpu as pltpu
from jax.sharding import PartitionSpec as P

LANES = 128
HALO = 8
WIDE = 512
SLICE = 256
EDGE = 16
PAIR = 2
VMEM_BYTES = 52 * 1024 * 1024
MESH = pl.DeviceIdType.MESH
F32 = jnp.float32
BF16 = jnp.bfloat16


def labels(position, starts, flag, length):
    position = jnp.minimum(position, length - 1)
    label = (flag[0] == 0).astype(jnp.int32)
    label = label + (starts[0, 0] <= position).astype(jnp.int32)
    label = label + (starts[0, 1] <= position).astype(jnp.int32)
    return jnp.where(position < 0, 0, label)


def layer(
    count, summed, short_scale, med_scale,
    starts, flag, q_ref, k_ref, v_ref, og_ref, w_ref, taps_ref, turned_ref,
    gated_ref, gq_ref, gk_ref, gv_ref, sums_ref,
    qf_ref, kf_ref, vf_ref, mixed_ref, grad_ref, short_ref,
    tail_out, tail_in, mixed_out, mixed_in, grad_out, grad_in, head_out, head_in, part, slots,
    back_masks, fore_masks, masks, rev_masks, back, ext, left, left_t, left_p, prod, prod_t, prod_p,
    tail_send, tail_recv, mixed_send, mixed_recv, grad_send, grad_recv, head_send, head_recv,
    part_send, part_recv, sum_send, sum_recv,
):
    length, channels = q_ref.shape
    fir_len = w_ref.shape[0]
    size = channels // taps_ref.shape[0]
    per_tile = LANES // size
    chunks = channels // WIDE
    tiles = WIDE // LANES
    slices = WIDE // SLICE
    me = lax.axis_index("ctx")
    has_before, has_after = me > 0, me < count - 1
    before, after = jnp.maximum(me - 1, 0), jnp.minimum(me + 1, count - 1)
    signals = (q_ref, k_ref, v_ref)

    def copy(src, dst, send, recv, peer):
        return pltpu.make_async_remote_copy(
            src_ref=src, dst_ref=dst, send_sem=send, recv_sem=recv, device_id={"ctx": peer}, device_id_type=MESH
        )

    def tail_copy():
        return copy(tail_out, tail_in, tail_send, tail_recv, after)

    def mixed_copy(c):
        return copy(mixed_out.at[c], mixed_in.at[c], mixed_send.at[c], mixed_recv.at[c], after)

    def grad_copy(c):
        return copy(grad_out.at[c], grad_in.at[c], grad_send.at[c], grad_recv.at[c], before)

    def head_copy(c):
        return copy(head_out.at[c], head_in.at[c], head_send.at[c], head_recv.at[c], before)

    barrier = pltpu.get_barrier_semaphore()

    def greet(peer):
        pl.semaphore_signal(barrier, inc=1, device_id={"ctx": peer}, device_id_type=MESH)

    if summed:
        for d in range(1, count):
            greet(lax.rem(me + d, count))
    else:
        pl.when(has_before)(lambda: greet(before))
        pl.when(has_after)(lambda: greet(after))

    def label(position):
        return labels(position, starts, flag, length)

    edge_row = lax.broadcasted_iota(jnp.int32, (EDGE, channels), 0) + (length - EDGE)
    edge_mask = (label(edge_row) == label(edge_row * 0 + (length - 1))).astype(F32)
    for n, x in enumerate(signals):
        tail_out[n] = (x[length - EDGE :, :].astype(F32) * edge_mask).astype(BF16)

    if summed:
        pl.semaphore_wait(barrier, count - 1)
    else:
        pl.when(has_before)(lambda: pl.semaphore_wait(barrier, 1))
        pl.when(has_after)(lambda: pl.semaphore_wait(barrier, 1))

    @pl.when(has_after)
    def _():
        tail_copy().start()

    row = lax.broadcasted_iota(jnp.int32, (length, LANES), 0)
    col = lax.broadcasted_iota(jnp.int32, (length, LANES), 1)
    own = label(row)
    across = label(col)
    last = label(row * 0 + (length - 1))
    for j in range(fir_len):
        back_masks[j] = (label(row - j) == own).astype(F32)
        fore_masks[j] = (label(row + j) == own).astype(F32)
    back_masks[fir_len] = (own == last).astype(F32)
    back_masks[fir_len + 1] = (own == 0).astype(F32)
    masks[0] = ((col <= row) & (own == across)).astype(F32).astype(BF16)
    masks[1] = ((col > row) & (own == 0)).astype(F32).astype(BF16)
    masks[2] = ((col >= row) & (own == across)).astype(F32).astype(BF16)
    masks[3] = ((col < row) & (own == last)).astype(F32).astype(BF16)
    rev = (length - 1) - row
    rev_masks[0] = ((col <= rev) & (label(rev) == across)).astype(F32)
    rev_masks[1] = ((col > rev) & (label(rev) == 0)).astype(F32)
    back[...] = (row + col == length - 1).astype(F32).astype(BF16)
    group_of_lane = col // size

    @pl.when(me == 0)
    def _():
        tail_in[...] = jnp.zeros(tail_in.shape, BF16)
        mixed_in[...] = jnp.zeros(mixed_in.shape, BF16)

    @pl.when(me == count - 1)
    def _():
        grad_in[...] = jnp.zeros(grad_in.shape, BF16)
        head_in[...] = jnp.zeros(head_in.shape, BF16)

    @pl.when(has_before)
    def _():
        tail_copy().wait_recv()

    def lanes(start):
        return pl.ds(pl.multiple_of(start, LANES), LANES)

    def forward_chunk(c, carry):
        def tile(i, carry):
            inner = lanes(i * LANES)
            start = c * WIDE + i * LANES
            cols = lanes(start)
            filtered = []
            for n, (x, out) in enumerate(((q_ref, qf_ref), (k_ref, kf_ref), (v_ref, vf_ref))):
                ext[n, :HALO, :] = tail_in[n, :, cols].astype(F32)[EDGE - HALO :]
                ext[n, HALO : HALO + length, :] = x[:, cols].astype(F32)
                weight = w_ref[:, lanes(n * channels + start)]
                total = weight[0:1] * ext[n, HALO : HALO + length, :]
                for j in range(1, fir_len):
                    total = total + weight[j : j + 1] * (ext[n, HALO - j : HALO - j + length, :] * back_masks[j])
                out[:, cols] = total
                filtered.append(total)
            query, key, value = filtered
            mixed = (key * value).astype(BF16)
            mixed_ref[:, cols] = mixed
            mixed_out[c, :, inner] = (mixed.astype(F32) * back_masks[fir_len]).astype(BF16)
            grad = (og_ref[:, cols].astype(F32) * query).astype(BF16)
            grad_ref[:, cols] = grad
            grad_out[c, :, inner] = (grad.astype(F32) * back_masks[fir_len + 1]).astype(BF16)
            return carry

        lax.fori_loop(0, tiles, tile, 0)
        pl.when(has_after)(lambda: mixed_copy(c).start())
        pl.when(has_before)(lambda: grad_copy(c).start())
        return carry

    lax.fori_loop(0, chunks, forward_chunk, 0)

    def long_tile(c, i, u):
        inner = lanes(i * LANES)
        start = c * WIDE + i * LANES
        cols = lanes(start)
        rows = pl.ds(pl.multiple_of((c * tiles + i) * per_tile, per_tile), per_tile)
        taps = taps_ref[rows, :]
        turned = turned_ref[rows, :]
        grad = grad_ref[:, cols]
        both = jnp.concatenate([mixed_ref[:, cols], mixed_in[c, :, inner]], axis=0)
        both_grad = jnp.concatenate([grad, grad_in[c, :, inner]], axis=0)
        flipped = jnp.dot(back[...], grad, preferred_element_type=F32)
        for g in range(per_tile):
            here = slice(g * length, (g + 1) * length)
            ring = pltpu.roll(
                jnp.broadcast_to(turned[g : g + 1], (length, length)), 0, 1, stride=1, stride_axis=0
            ).astype(BF16)
            left[u, here, :length] = ring * masks[0]
            left[u, here, length:] = ring * masks[1]
            ring_t = pltpu.roll(
                jnp.broadcast_to(taps[g : g + 1], (length, length)), 0, 1, stride=1, stride_axis=0
            ).astype(BF16)
            left_t[u, here, :length] = ring_t * masks[2]
            left_t[u, here, length:] = ring_t * masks[3]
            left_p[u, here, :] = jnp.where(group_of_lane == g, flipped, 0.0).astype(BF16)
        prod[u] = jnp.dot(left[u], both, preferred_element_type=F32)
        prod_t[u] = jnp.dot(left_t[u], both_grad, preferred_element_type=F32)
        prod_p[u] = lax.dot_general(left_p[u], both, (((1,), (1,)), ((), ())), preferred_element_type=F32)
        conv = prod[u, :length, :]
        mixed_grad = prod_t[u, :length, :]
        sums = []
        for g in range(per_tile):
            here = slice(g * length, (g + 1) * length)
            if g:
                conv = jnp.where(group_of_lane == g, prod[u, here, :], conv)
                mixed_grad = jnp.where(group_of_lane == g, prod_t[u, here, :], mixed_grad)
            pair = prod_p[u, here, :length] * rev_masks[0] + prod_p[u, here, length:] * rev_masks[1]
            pair = pltpu.roll(pair, 0, 1, stride=1, stride_axis=0)
            sums.append(jnp.sum(pair, axis=0, keepdims=True))
        part[c * slices + i // PAIR, 3 * HALO :, u * LANES : (u + 1) * LANES] = jnp.concatenate(sums, axis=0)
        gated_ref[:, cols] = (qf_ref[:, cols] * conv).astype(BF16)
        products = (
            og_ref[:, cols].astype(F32) * conv, mixed_grad * vf_ref[:, cols], mixed_grad * kf_ref[:, cols],
        )
        for n, product in enumerate(products):
            rounded = product.astype(BF16)
            short_ref[n, :, cols] = rounded
            edge = rounded[:EDGE].astype(F32) * back_masks[fir_len + 1, :EDGE, :]
            head_out[c, n, :, inner] = edge.astype(BF16)

    def long_chunk(c, carry):
        pl.when(has_before)(lambda: mixed_copy(c).wait_recv())
        pl.when(has_after)(lambda: grad_copy(c).wait_recv())

        def pair(i, carry):
            for u in range(PAIR):
                long_tile(c, i * PAIR + u, u)
            return carry

        lax.fori_loop(0, tiles // PAIR, pair, 0)
        pl.when(has_before)(lambda: head_copy(c).start())
        return carry

    lax.fori_loop(0, chunks, long_chunk, 0)

    def part_copy(target, source):
        return copy(part.at[target], slots.at[source], part_send.at[target], part_recv.at[source], target)

    def backward_chunk(c, carry):
        pl.when(has_after)(lambda: head_copy(c).wait_recv())

        def pair(i, carry):
            for u in range(PAIR):
                inner = lanes((i * PAIR + u) * LANES)
                start = c * WIDE + (i * PAIR + u) * LANES
                cols = lanes(start)
                for n, (x, out) in enumerate(((q_ref, gq_ref), (k_ref, gk_ref), (v_ref, gv_ref))):
                    e = u * 3 + n
                    ext[e, :length, :] = short_ref[n, :, cols].astype(F32)
                    ext[e, length : length + HALO, :] = head_in[c, n, :, inner].astype(F32)[:HALO]
                    weight = w_ref[:, lanes(n * channels + start)]
                    signal = x[:, cols].astype(F32)
                    total = None
                    sums = []
                    for j in range(fir_len):
                        moved = ext[e, j : j + length, :]
                        if j:
                            moved = moved * fore_masks[j]
                        term = weight[j : j + 1] * moved
                        total = term if total is None else total + term
                        sums.append(jnp.sum(signal * moved, axis=0, keepdims=True))
                    sums.append(jnp.zeros((HALO - fir_len, LANES), F32))
                    out[:, cols] = total.astype(BF16)
                    part[c * slices + i, n * HALO : (n + 1) * HALO, u * LANES : (u + 1) * LANES] = jnp.concatenate(
                        sums, axis=0
                    )
            return carry

        lax.fori_loop(0, slices, pair, 0)
        if summed:
            for s in range(slices):
                target = c * slices + s

                @pl.when(target != me)
                def _():
                    part_copy(target, me).start()

        return carry

    lax.fori_loop(0, chunks, backward_chunk, 0)

    if summed:
        def add(d, total):
            source = lax.rem(me + d, count)
            part_copy(me, source).wait_recv()
            return total + slots[source]

        total = lax.fori_loop(1, count, add, part[me])
        kind = lax.broadcasted_iota(jnp.int32, total.shape, 0)
        sums_ref[me] = total * jnp.where(kind < 3 * HALO, short_scale, med_scale)
        core = lax.rem(me, 2)
        other = me + 1 - 2 * core

        def sum_copy(slot, way, peer):
            return copy(sums_ref.at[slot], sums_ref.at[slot], sum_send.at[way], sum_recv.at[slot], peer)

        chips = count // 2
        for d in range(1, chips):
            sum_copy(me, d, lax.rem(me + 2 * d, count)).start()
        sum_copy(me, 0, other).start()
        for d in range(1, chips):
            slot = lax.rem(me + count - 2 * d, count)
            sum_copy(slot, d, other).wait_recv()
            sum_copy(slot, chips + d, other).start()
        for d in range(chips):
            slot = lax.rem(other + count - 2 * d, count)
            sum_copy(slot, d, other).wait_recv()
        for d in range(1, chips):
            sum_copy(me, d, lax.rem(me + 2 * d, count)).wait_send()
            sum_copy(me, chips + d, other).wait_send()
        sum_copy(me, 0, other).wait_send()

        def drain(d, carry):
            part_copy(lax.rem(me + d, count), me).wait_send()
            return carry

        lax.fori_loop(1, count, drain, 0)
    else:
        sums_ref[...] = part[...]

    @pl.when(has_after)
    def _():
        tail_copy().wait_send()

    def finish(c, carry):
        @pl.when(has_after)
        def _():
            mixed_copy(c).wait_send()

        @pl.when(has_before)
        def _():
            grad_copy(c).wait_send()
            head_copy(c).wait_send()

        return carry

    lax.fori_loop(0, chunks, finish, 0)


def local(query_proj, key_proj, value_proj, out_grad, short_taps, medium_taps, doc_starts, continues):
    length, channels = query_proj.shape
    groups, med_len = medium_taps.shape
    size = channels // groups
    per_tile = LANES // size
    fir_len = short_taps.shape[0]
    count = lax.axis_size("ctx")
    chunks, pieces = channels // WIDE, channels // SLICE
    summed = pieces == count
    tokens = length * count
    short_scale = 1.0 / math.sqrt(tokens)
    med_scale = 1.0 / math.sqrt(tokens * size)
    taps_f = short_taps.astype(F32)
    med_f = medium_taps.astype(F32)
    turned = jnp.roll(jnp.flip(med_f, axis=1), 1, axis=1)
    shape = jax.ShapeDtypeStruct
    half = shape((length, channels), BF16)
    vmem = pl.BlockSpec(memory_space=pltpu.VMEM)
    smem = pl.BlockSpec(memory_space=pltpu.SMEM)
    dma = pltpu.SemaphoreType.DMA
    buffer = pltpu.VMEM
    gated, gq, gk, gv, sums = pl.pallas_call(
        functools.partial(layer, count, summed, short_scale, med_scale),
        in_specs=[smem] * 2 + [vmem] * 7,
        out_specs=[vmem] * 5,
        out_shape=[half] * 4 + [shape((pieces, 4 * HALO, SLICE), F32)],
        scratch_shapes=[buffer((length, channels), F32)] * 3
        + [buffer((length, channels), BF16)] * 2
        + [buffer((3, length, channels), BF16)]
        + [buffer((3, EDGE, channels), BF16)] * 2
        + [buffer((chunks, length, WIDE), BF16)] * 4
        + [buffer((chunks, 3, EDGE, WIDE), BF16)] * 2
        + [buffer((pieces, 4 * HALO, SLICE), F32)] * 2
        + [
            buffer((fir_len + 2, length, LANES), F32),
            buffer((fir_len, length, LANES), F32),
            buffer((4, length, length), BF16),
            buffer((2, length, length), F32),
            buffer((length, length), BF16),
            buffer((3 * PAIR, length + HALO, LANES), F32),
            buffer((PAIR, per_tile * length, 2 * length), BF16),
            buffer((PAIR, per_tile * length, 2 * length), BF16),
            buffer((PAIR, per_tile * length, LANES), BF16),
            buffer((PAIR, per_tile * length, LANES), F32),
            buffer((PAIR, per_tile * length, LANES), F32),
            buffer((PAIR, per_tile * length, 2 * length), F32),
        ]
        + [dma(())] * 2
        + [dma((chunks,))] * 6
        + [dma((count,))] * 4,
        compiler_params=pltpu.CompilerParams(
            vmem_limit_bytes=VMEM_BYTES, collective_id=0, has_side_effects=True
        ),
    )(doc_starts, continues, query_proj, key_proj, value_proj, out_grad, taps_f, med_f, turned)
    if not summed:
        sums = lax.psum(sums, "ctx")
        sums = jnp.concatenate([sums[:, : 3 * HALO] * short_scale, sums[:, 3 * HALO :] * med_scale], axis=1)
    short = sums[:, : 3 * HALO].reshape(pieces, 3, HALO, SLICE)[:, :, :fir_len]
    grad_short = short.transpose(2, 1, 0, 3).reshape(fir_len, 3 * channels)
    medium = sums[:, 3 * HALO :].reshape(pieces, HALO, SLICE // LANES, LANES).transpose(0, 2, 1, 3)
    grad_medium = jnp.flip(medium.reshape(groups, med_len), axis=1)
    return gated, gq, gk, gv, grad_short, grad_medium


def solution(mesh):
    tokens = P(("grp", "ctx"), None)
    in_specs = (tokens,) * 4 + (P(), P(), tokens, P(("grp", "ctx")))
    out_specs = (tokens,) * 4 + (P("grp", None), P("grp", None))
    return jax.shard_map(local, mesh=mesh, in_specs=in_specs, out_specs=out_specs, check_vma=False)
```

```python
import functools
import math

import jax
import jax.numpy as jnp
from jax import lax
from jax.experimental import pallas as pl
from jax.experimental.pallas import tpu as pltpu
from jax.sharding import PartitionSpec as P

LANES = 128
HALO = 8
WIDE = 512
SLICE = 256
EDGE = 16
PAIR = 2
VMEM_BYTES = 52 * 1024 * 1024
MESH = pl.DeviceIdType.MESH
F32 = jnp.float32
BF16 = jnp.bfloat16


def labels(position, starts, flag, length):
    position = jnp.minimum(position, length - 1)
    label = (flag[0] == 0).astype(jnp.int32)
    label = label + (starts[0, 0] <= position).astype(jnp.int32)
    label = label + (starts[0, 1] <= position).astype(jnp.int32)
    return jnp.where(position < 0, 0, label)


def layer(
    count, summed, short_scale, med_scale,
    starts, flag, q_ref, k_ref, v_ref, og_ref, w_ref, taps_ref, turned_ref,
    gated_out, gq_out, gk_out, gv_out, sums_ref,
    gated_ref, gq_ref, gk_ref, gv_ref, qf_ref, kf_ref, vf_ref, mixed_ref, grad_ref, short_ref,
    tail_out, tail_in, mixed_out, mixed_in, grad_out, grad_in, head_out, head_in, part, slots,
    back_masks, fore_masks, masks, rev_masks, back, ext, left, left_t, left_p, prod, prod_t, prod_p,
    tail_send, tail_recv, mixed_send, mixed_recv, grad_send, grad_recv, head_send, head_recv,
    part_send, part_recv, sum_send, sum_recv, store_sem,
):
    length, channels = q_ref.shape
    fir_len = w_ref.shape[0]
    size = channels // taps_ref.shape[0]
    per_tile = LANES // size
    chunks = channels // WIDE
    tiles = WIDE // LANES
    slices = WIDE // SLICE
    me = lax.axis_index("ctx")
    has_before, has_after = me > 0, me < count - 1
    before, after = jnp.maximum(me - 1, 0), jnp.minimum(me + 1, count - 1)
    signals = (q_ref, k_ref, v_ref)

    def copy(src, dst, send, recv, peer):
        return pltpu.make_async_remote_copy(
            src_ref=src, dst_ref=dst, send_sem=send, recv_sem=recv, device_id={"ctx": peer}, device_id_type=MESH
        )

    def tail_copy():
        return copy(tail_out, tail_in, tail_send, tail_recv, after)

    def mixed_copy(c):
        return copy(mixed_out.at[c], mixed_in.at[c], mixed_send.at[c], mixed_recv.at[c], after)

    def grad_copy(c):
        return copy(grad_out.at[c], grad_in.at[c], grad_send.at[c], grad_recv.at[c], before)

    def head_copy(c):
        return copy(head_out.at[c], head_in.at[c], head_send.at[c], head_recv.at[c], before)

    barrier = pltpu.get_barrier_semaphore()

    def greet(peer):
        pl.semaphore_signal(barrier, inc=1, device_id={"ctx": peer}, device_id_type=MESH)

    if summed:
        for d in range(1, count):
            greet(lax.rem(me + d, count))
    else:
        pl.when(has_before)(lambda: greet(before))
        pl.when(has_after)(lambda: greet(after))

    def label(position):
        return labels(position, starts, flag, length)

    edge_row = lax.broadcasted_iota(jnp.int32, (EDGE, channels), 0) + (length - EDGE)
    edge_mask = (label(edge_row) == label(edge_row * 0 + (length - 1))).astype(F32)
    for n, x in enumerate(signals):
        tail_out[n] = (x[length - EDGE :, :].astype(F32) * edge_mask).astype(BF16)

    if summed:
        pl.semaphore_wait(barrier, count - 1)
    else:
        pl.when(has_before)(lambda: pl.semaphore_wait(barrier, 1))
        pl.when(has_after)(lambda: pl.semaphore_wait(barrier, 1))

    @pl.when(has_after)
    def _():
        tail_copy().start()

    row = lax.broadcasted_iota(jnp.int32, (length, LANES), 0)
    col = lax.broadcasted_iota(jnp.int32, (length, LANES), 1)
    own = label(row)
    across = label(col)
    last = label(row * 0 + (length - 1))
    for j in range(fir_len):
        back_masks[j] = (label(row - j) == own).astype(F32)
        fore_masks[j] = (label(row + j) == own).astype(F32)
    back_masks[fir_len] = (own == last).astype(F32)
    back_masks[fir_len + 1] = (own == 0).astype(F32)
    masks[0] = ((col <= row) & (own == across)).astype(F32).astype(BF16)
    masks[1] = ((col > row) & (own == 0)).astype(F32).astype(BF16)
    masks[2] = ((col >= row) & (own == across)).astype(F32).astype(BF16)
    masks[3] = ((col < row) & (own == last)).astype(F32).astype(BF16)
    rev = (length - 1) - row
    rev_masks[0] = ((col <= rev) & (label(rev) == across)).astype(F32)
    rev_masks[1] = ((col > rev) & (label(rev) == 0)).astype(F32)
    back[...] = (row + col == length - 1).astype(F32).astype(BF16)
    group_of_lane = col // size

    @pl.when(me == 0)
    def _():
        tail_in[...] = jnp.zeros(tail_in.shape, BF16)
        mixed_in[...] = jnp.zeros(mixed_in.shape, BF16)

    @pl.when(me == count - 1)
    def _():
        grad_in[...] = jnp.zeros(grad_in.shape, BF16)
        head_in[...] = jnp.zeros(head_in.shape, BF16)

    @pl.when(has_before)
    def _():
        tail_copy().wait_recv()

    def lanes(start):
        return pl.ds(pl.multiple_of(start, LANES), LANES)

    def forward_chunk(c, carry):
        def tile(i, carry):
            inner = lanes(i * LANES)
            start = c * WIDE + i * LANES
            cols = lanes(start)
            filtered = []
            for n, (x, out) in enumerate(((q_ref, qf_ref), (k_ref, kf_ref), (v_ref, vf_ref))):
                ext[n, :HALO, :] = tail_in[n, :, cols].astype(F32)[EDGE - HALO :]
                ext[n, HALO : HALO + length, :] = x[:, cols].astype(F32)
                weight = w_ref[:, lanes(n * channels + start)]
                total = weight[0:1] * ext[n, HALO : HALO + length, :]
                for j in range(1, fir_len):
                    total = total + weight[j : j + 1] * (ext[n, HALO - j : HALO - j + length, :] * back_masks[j])
                out[:, cols] = total
                filtered.append(total)
            query, key, value = filtered
            mixed = (key * value).astype(BF16)
            mixed_ref[:, cols] = mixed
            mixed_out[c, :, inner] = (mixed.astype(F32) * back_masks[fir_len]).astype(BF16)
            grad = (og_ref[:, cols].astype(F32) * query).astype(BF16)
            grad_ref[:, cols] = grad
            grad_out[c, :, inner] = (grad.astype(F32) * back_masks[fir_len + 1]).astype(BF16)
            return carry

        lax.fori_loop(0, tiles, tile, 0)
        pl.when(has_after)(lambda: mixed_copy(c).start())
        pl.when(has_before)(lambda: grad_copy(c).start())
        return carry

    lax.fori_loop(0, chunks, forward_chunk, 0)

    def long_tile(c, i, u):
        inner = lanes(i * LANES)
        start = c * WIDE + i * LANES
        cols = lanes(start)
        rows = pl.ds(pl.multiple_of((c * tiles + i) * per_tile, per_tile), per_tile)
        taps = taps_ref[rows, :]
        turned = turned_ref[rows, :]
        grad = grad_ref[:, cols]
        both = jnp.concatenate([mixed_ref[:, cols], mixed_in[c, :, inner]], axis=0)
        both_grad = jnp.concatenate([grad, grad_in[c, :, inner]], axis=0)
        flipped = jnp.dot(back[...], grad, preferred_element_type=F32)
        for g in range(per_tile):
            here = slice(g * length, (g + 1) * length)
            ring = pltpu.roll(
                jnp.broadcast_to(turned[g : g + 1], (length, length)), 0, 1, stride=1, stride_axis=0
            ).astype(BF16)
            left[u, here, :length] = ring * masks[0]
            left[u, here, length:] = ring * masks[1]
            ring_t = pltpu.roll(
                jnp.broadcast_to(taps[g : g + 1], (length, length)), 0, 1, stride=1, stride_axis=0
            ).astype(BF16)
            left_t[u, here, :length] = ring_t * masks[2]
            left_t[u, here, length:] = ring_t * masks[3]
            left_p[u, here, :] = jnp.where(group_of_lane == g, flipped, 0.0).astype(BF16)
        prod[u] = jnp.dot(left[u], both, preferred_element_type=F32)
        prod_t[u] = jnp.dot(left_t[u], both_grad, preferred_element_type=F32)
        prod_p[u] = lax.dot_general(left_p[u], both, (((1,), (1,)), ((), ())), preferred_element_type=F32)
        conv = prod[u, :length, :]
        mixed_grad = prod_t[u, :length, :]
        sums = []
        for g in range(per_tile):
            here = slice(g * length, (g + 1) * length)
            if g:
                conv = jnp.where(group_of_lane == g, prod[u, here, :], conv)
                mixed_grad = jnp.where(group_of_lane == g, prod_t[u, here, :], mixed_grad)
            pair = prod_p[u, here, :length] * rev_masks[0] + prod_p[u, here, length:] * rev_masks[1]
            pair = pltpu.roll(pair, 0, 1, stride=1, stride_axis=0)
            sums.append(jnp.sum(pair, axis=0, keepdims=True))
        part[c * slices + i // PAIR, 3 * HALO :, u * LANES : (u + 1) * LANES] = jnp.concatenate(sums, axis=0)
        gated_ref[:, cols] = (qf_ref[:, cols] * conv).astype(BF16)
        products = (
            og_ref[:, cols].astype(F32) * conv, mixed_grad * vf_ref[:, cols], mixed_grad * kf_ref[:, cols],
        )
        for n, product in enumerate(products):
            rounded = product.astype(BF16)
            short_ref[n, :, cols] = rounded
            edge = rounded[:EDGE].astype(F32) * back_masks[fir_len + 1, :EDGE, :]
            head_out[c, n, :, inner] = edge.astype(BF16)

    def long_chunk(c, carry):
        pl.when(has_before)(lambda: mixed_copy(c).wait_recv())
        pl.when(has_after)(lambda: grad_copy(c).wait_recv())

        def pair(i, carry):
            for u in range(PAIR):
                long_tile(c, i * PAIR + u, u)
            return carry

        lax.fori_loop(0, tiles // PAIR, pair, 0)
        pl.when(has_before)(lambda: head_copy(c).start())
        return carry

    lax.fori_loop(0, chunks, long_chunk, 0)
    stores = [
        pltpu.make_async_copy(src, dst, store_sem.at[n])
        for n, (src, dst) in enumerate(
            ((gated_ref, gated_out), (gq_ref, gq_out), (gk_ref, gk_out), (gv_ref, gv_out))
        )
    ]
    stores[0].start()

    def part_copy(target, source):
        return copy(part.at[target], slots.at[source], part_send.at[target], part_recv.at[source], target)

    def backward_chunk(step, carry):
        c = lax.rem(step + 1 + me // slices, chunks)
        pl.when(has_after)(lambda: head_copy(c).wait_recv())

        def pair(i, carry):
            for u in range(PAIR):
                inner = lanes((i * PAIR + u) * LANES)
                start = c * WIDE + (i * PAIR + u) * LANES
                cols = lanes(start)
                for n, (x, out) in enumerate(((q_ref, gq_ref), (k_ref, gk_ref), (v_ref, gv_ref))):
                    e = u * 3 + n
                    ext[e, :length, :] = short_ref[n, :, cols].astype(F32)
                    ext[e, length : length + HALO, :] = head_in[c, n, :, inner].astype(F32)[:HALO]
                    weight = w_ref[:, lanes(n * channels + start)]
                    signal = x[:, cols].astype(F32)
                    total = None
                    sums = []
                    for j in range(fir_len):
                        moved = ext[e, j : j + length, :]
                        if j:
                            moved = moved * fore_masks[j]
                        term = weight[j : j + 1] * moved
                        total = term if total is None else total + term
                        sums.append(jnp.sum(signal * moved, axis=0, keepdims=True))
                    sums.append(jnp.zeros((HALO - fir_len, LANES), F32))
                    out[:, cols] = total.astype(BF16)
                    part[c * slices + i, n * HALO : (n + 1) * HALO, u * LANES : (u + 1) * LANES] = jnp.concatenate(
                        sums, axis=0
                    )
            return carry

        lax.fori_loop(0, slices, pair, 0)
        if summed:
            for s in range(slices):
                target = c * slices + s

                @pl.when(target != me)
                def _():
                    part_copy(target, me).start()

        return carry

    lax.fori_loop(0, chunks, backward_chunk, 0)
    for store in stores[1:]:
        store.start()

    if summed:
        def add(d, total):
            source = lax.rem(me + d, count)
            part_copy(me, source).wait_recv()
            return total + slots[source]

        total = lax.fori_loop(1, count, add, part[me])
        kind = lax.broadcasted_iota(jnp.int32, total.shape, 0)
        sums_ref[me] = total * jnp.where(kind < 3 * HALO, short_scale, med_scale)
        core = lax.rem(me, 2)
        other = me + 1 - 2 * core

        def sum_copy(slot, way, peer):
            return copy(sums_ref.at[slot], sums_ref.at[slot], sum_send.at[way], sum_recv.at[slot], peer)

        chips = count // 2
        for d in range(1, chips):
            sum_copy(me, d, lax.rem(me + 2 * d, count)).start()
        sum_copy(me, 0, other).start()
        for d in range(1, chips):
            slot = lax.rem(me + count - 2 * d, count)
            sum_copy(slot, d, other).wait_recv()
            sum_copy(slot, chips + d, other).start()
        for d in range(chips):
            slot = lax.rem(other + count - 2 * d, count)
            sum_copy(slot, d, other).wait_recv()
        for d in range(1, chips):
            sum_copy(me, d, lax.rem(me + 2 * d, count)).wait_send()
            sum_copy(me, chips + d, other).wait_send()
        sum_copy(me, 0, other).wait_send()

        def drain(d, carry):
            part_copy(lax.rem(me + d, count), me).wait_send()
            return carry

        lax.fori_loop(1, count, drain, 0)
    else:
        sums_ref[...] = part[...]

    @pl.when(has_after)
    def _():
        tail_copy().wait_send()

    def finish(c, carry):
        @pl.when(has_after)
        def _():
            mixed_copy(c).wait_send()

        @pl.when(has_before)
        def _():
            grad_copy(c).wait_send()
            head_copy(c).wait_send()

        return carry

    lax.fori_loop(0, chunks, finish, 0)
    for store in stores:
        store.wait()


def local(query_proj, key_proj, value_proj, out_grad, short_taps, medium_taps, doc_starts, continues):
    length, channels = query_proj.shape
    groups, med_len = medium_taps.shape
    size = channels // groups
    per_tile = LANES // size
    fir_len = short_taps.shape[0]
    count = lax.axis_size("ctx")
    chunks, pieces = channels // WIDE, channels // SLICE
    summed = pieces == count
    tokens = length * count
    short_scale = 1.0 / math.sqrt(tokens)
    med_scale = 1.0 / math.sqrt(tokens * size)
    taps_f = short_taps.astype(F32)
    med_f = medium_taps.astype(F32)
    turned = jnp.roll(jnp.flip(med_f, axis=1), 1, axis=1)
    shape = jax.ShapeDtypeStruct
    half = shape((length, channels), BF16)
    vmem = pl.BlockSpec(memory_space=pltpu.VMEM)
    smem = pl.BlockSpec(memory_space=pltpu.SMEM)
    dma = pltpu.SemaphoreType.DMA
    buffer = pltpu.VMEM
    gated, gq, gk, gv, sums = pl.pallas_call(
        functools.partial(layer, count, summed, short_scale, med_scale),
        in_specs=[smem] * 2 + [vmem] * 7,
        out_specs=[pl.BlockSpec(memory_space=pl.ANY)] * 4 + [vmem],
        out_shape=[half] * 4 + [shape((pieces, 4 * HALO, SLICE), F32)],
        scratch_shapes=[buffer((length, channels), BF16)] * 4
        + [buffer((length, channels), F32)] * 3
        + [buffer((length, channels), BF16)] * 2
        + [buffer((3, length, channels), BF16)]
        + [buffer((3, EDGE, channels), BF16)] * 2
        + [buffer((chunks, length, WIDE), BF16)] * 4
        + [buffer((chunks, 3, EDGE, WIDE), BF16)] * 2
        + [buffer((pieces, 4 * HALO, SLICE), F32)] * 2
        + [
            buffer((fir_len + 2, length, LANES), F32),
            buffer((fir_len, length, LANES), F32),
            buffer((4, length, length), BF16),
            buffer((2, length, length), F32),
            buffer((length, length), BF16),
            buffer((3 * PAIR, length + HALO, LANES), F32),
            buffer((PAIR, per_tile * length, 2 * length), BF16),
            buffer((PAIR, per_tile * length, 2 * length), BF16),
            buffer((PAIR, per_tile * length, LANES), BF16),
            buffer((PAIR, per_tile * length, LANES), F32),
            buffer((PAIR, per_tile * length, LANES), F32),
            buffer((PAIR, per_tile * length, 2 * length), F32),
        ]
        + [dma(())] * 2
        + [dma((chunks,))] * 6
        + [dma((count,))] * 4
        + [dma((4,))],
        compiler_params=pltpu.CompilerParams(
            vmem_limit_bytes=VMEM_BYTES, collective_id=0, has_side_effects=True
        ),
    )(doc_starts, continues, query_proj, key_proj, value_proj, out_grad, taps_f, med_f, turned)
    if not summed:
        sums = lax.psum(sums, "ctx")
        sums = jnp.concatenate([sums[:, : 3 * HALO] * short_scale, sums[:, 3 * HALO :] * med_scale], axis=1)
    short = sums[:, : 3 * HALO].reshape(pieces, 3, HALO, SLICE)[:, :, :fir_len]
    grad_short = short.transpose(2, 1, 0, 3).reshape(fir_len, 3 * channels)
    medium = sums[:, 3 * HALO :].reshape(pieces, HALO, SLICE // LANES, LANES).transpose(0, 2, 1, 3)
    grad_medium = jnp.flip(medium.reshape(groups, med_len), axis=1)
    return gated, gq, gk, gv, grad_short, grad_medium


def solution(mesh):
    tokens = P(("grp", "ctx"), None)
    in_specs = (tokens,) * 4 + (P(), P(), tokens, P(("grp", "ctx")))
    out_specs = (tokens,) * 4 + (P("grp", None), P("grp", None))
    return jax.shard_map(local, mesh=mesh, in_specs=in_specs, out_specs=out_specs, check_vma=False)
```

```python
import functools
import math

import jax
import jax.numpy as jnp
from jax import lax
from jax.experimental import pallas as pl
from jax.experimental.pallas import tpu as pltpu
from jax.sharding import PartitionSpec as P

LANES = 128
HALO = 8
WIDE = 512
SLICE = 256
EDGE = 16
PAIR = 2
VMEM_BYTES = 52 * 1024 * 1024
MESH = pl.DeviceIdType.MESH
F32 = jnp.float32
BF16 = jnp.bfloat16


def labels(position, starts, flag, length):
    position = jnp.minimum(position, length - 1)
    label = (flag[0] == 0).astype(jnp.int32)
    label = label + (starts[0, 0] <= position).astype(jnp.int32)
    label = label + (starts[0, 1] <= position).astype(jnp.int32)
    return jnp.where(position < 0, 0, label)


def layer(
    count, summed, short_scale, med_scale,
    starts, flag, q_ref, k_ref, v_ref, og_ref, w_ref, taps_ref, turned_ref,
    gated_out, gq_out, gk_out, gv_out, sums_ref,
    gated_ref, gq_ref, gk_ref, gv_ref, qf_ref, kf_ref, vf_ref, mixed_ref, grad_ref, short_ref,
    tail_out, tail_in, mixed_out, mixed_in, grad_out, grad_in, head_out, head_in, part, slots,
    back_masks, fore_masks, masks, rev_masks, back, ext, left, left_t, left_p, prod, prod_t, prod_p,
    tail_send, tail_recv, mixed_send, mixed_recv, grad_send, grad_recv, head_send, head_recv,
    part_send, part_recv, sum_send, sum_recv, store_sem,
):
    length, channels = q_ref.shape
    fir_len = w_ref.shape[0]
    size = channels // taps_ref.shape[0]
    per_tile = LANES // size
    chunks = channels // WIDE
    tiles = WIDE // LANES
    slices = WIDE // SLICE
    me = lax.axis_index("ctx")
    has_before, has_after = me > 0, me < count - 1
    before, after = jnp.maximum(me - 1, 0), jnp.minimum(me + 1, count - 1)
    signals = (q_ref, k_ref, v_ref)

    def copy(src, dst, send, recv, peer):
        return pltpu.make_async_remote_copy(
            src_ref=src, dst_ref=dst, send_sem=send, recv_sem=recv, device_id={"ctx": peer}, device_id_type=MESH
        )

    def tail_copy():
        return copy(tail_out, tail_in, tail_send, tail_recv, after)

    def mixed_copy(c):
        return copy(mixed_out.at[c], mixed_in.at[c], mixed_send.at[c], mixed_recv.at[c], after)

    def grad_copy(c):
        return copy(grad_out.at[c], grad_in.at[c], grad_send.at[c], grad_recv.at[c], before)

    def head_copy(c):
        return copy(head_out.at[c], head_in.at[c], head_send.at[c], head_recv.at[c], before)

    barrier = pltpu.get_barrier_semaphore()

    def greet(peer):
        pl.semaphore_signal(barrier, inc=1, device_id={"ctx": peer}, device_id_type=MESH)

    if summed:
        for d in range(1, count):
            greet(lax.rem(me + d, count))
    else:
        pl.when(has_before)(lambda: greet(before))
        pl.when(has_after)(lambda: greet(after))

    def label(position):
        return labels(position, starts, flag, length)

    edge_row = lax.broadcasted_iota(jnp.int32, (EDGE, channels), 0) + (length - EDGE)
    edge_mask = (label(edge_row) == label(edge_row * 0 + (length - 1))).astype(F32)
    for n, x in enumerate(signals):
        tail_out[n] = (x[length - EDGE :, :].astype(F32) * edge_mask).astype(BF16)

    if summed:
        pl.semaphore_wait(barrier, count - 1)
    else:
        pl.when(has_before)(lambda: pl.semaphore_wait(barrier, 1))
        pl.when(has_after)(lambda: pl.semaphore_wait(barrier, 1))

    @pl.when(has_after)
    def _():
        tail_copy().start()

    row = lax.broadcasted_iota(jnp.int32, (length, LANES), 0)
    col = lax.broadcasted_iota(jnp.int32, (length, LANES), 1)
    own = label(row)
    across = label(col)
    last = label(row * 0 + (length - 1))
    for j in range(fir_len):
        back_masks[j] = (label(row - j) == own).astype(F32)
        fore_masks[j] = (label(row + j) == own).astype(F32)
    back_masks[fir_len] = (own == last).astype(F32)
    back_masks[fir_len + 1] = (own == 0).astype(F32)
    masks[0] = ((col <= row) & (own == across)).astype(F32).astype(BF16)
    masks[1] = ((col > row) & (own == 0)).astype(F32).astype(BF16)
    masks[2] = ((col >= row) & (own == across)).astype(F32).astype(BF16)
    masks[3] = ((col < row) & (own == last)).astype(F32).astype(BF16)
    rev = (length - 1) - row
    rev_masks[0] = ((col <= rev) & (label(rev) == across)).astype(F32)
    rev_masks[1] = ((col > rev) & (label(rev) == 0)).astype(F32)
    back[...] = (row + col == length - 1).astype(F32).astype(BF16)
    group_of_lane = col // size

    @pl.when(me == 0)
    def _():
        tail_in[...] = jnp.zeros(tail_in.shape, BF16)
        mixed_in[...] = jnp.zeros(mixed_in.shape, BF16)

    @pl.when(me == count - 1)
    def _():
        grad_in[...] = jnp.zeros(grad_in.shape, BF16)
        head_in[...] = jnp.zeros(head_in.shape, BF16)

    @pl.when(has_before)
    def _():
        tail_copy().wait_recv()

    def lanes(start):
        return pl.ds(pl.multiple_of(start, LANES), LANES)

    def forward_chunk(c, carry):
        def tile(i, u):
            inner = lanes(i * LANES)
            start = c * WIDE + i * LANES
            cols = lanes(start)
            filtered = []
            for n, (x, out) in enumerate(((q_ref, qf_ref), (k_ref, kf_ref), (v_ref, vf_ref))):
                ext[u * 3 + n, :HALO, :] = tail_in[n, :, cols].astype(F32)[EDGE - HALO :]
                ext[u * 3 + n, HALO : HALO + length, :] = x[:, cols].astype(F32)
                weight = w_ref[:, lanes(n * channels + start)]
                total = weight[0:1] * ext[u * 3 + n, HALO : HALO + length, :]
                for j in range(1, fir_len):
                    total = total + weight[j : j + 1] * (ext[u * 3 + n, HALO - j : HALO - j + length, :] * back_masks[j])
                out[:, cols] = total
                filtered.append(total)
            query, key, value = filtered
            mixed = (key * value).astype(BF16)
            mixed_ref[:, cols] = mixed
            mixed_out[c, :, inner] = (mixed.astype(F32) * back_masks[fir_len]).astype(BF16)
            grad = (og_ref[:, cols].astype(F32) * query).astype(BF16)
            grad_ref[:, cols] = grad
            grad_out[c, :, inner] = (grad.astype(F32) * back_masks[fir_len + 1]).astype(BF16)

        def pair(i, carry):
            for u in range(PAIR):
                tile(i * PAIR + u, u)
            return carry

        lax.fori_loop(0, tiles // PAIR, pair, 0)
        pl.when(has_after)(lambda: mixed_copy(c).start())
        pl.when(has_before)(lambda: grad_copy(c).start())
        return carry

    lax.fori_loop(0, chunks, forward_chunk, 0)

    def long_tile(c, i, u):
        inner = lanes(i * LANES)
        start = c * WIDE + i * LANES
        cols = lanes(start)
        rows = pl.ds(pl.multiple_of((c * tiles + i) * per_tile, per_tile), per_tile)
        taps = taps_ref[rows, :]
        turned = turned_ref[rows, :]
        grad = grad_ref[:, cols]
        both = jnp.concatenate([mixed_ref[:, cols], mixed_in[c, :, inner]], axis=0)
        both_grad = jnp.concatenate([grad, grad_in[c, :, inner]], axis=0)
        flipped = jnp.dot(back[...], grad, preferred_element_type=F32)
        for g in range(per_tile):
            here = slice(g * length, (g + 1) * length)
            ring = pltpu.roll(
                jnp.broadcast_to(turned[g : g + 1], (length, length)), 0, 1, stride=1, stride_axis=0
            ).astype(BF16)
            left[u, here, :length] = ring * masks[0]
            left[u, here, length:] = ring * masks[1]
            ring_t = pltpu.roll(
                jnp.broadcast_to(taps[g : g + 1], (length, length)), 0, 1, stride=1, stride_axis=0
            ).astype(BF16)
            left_t[u, here, :length] = ring_t * masks[2]
            left_t[u, here, length:] = ring_t * masks[3]
            left_p[u, here, :] = jnp.where(group_of_lane == g, flipped, 0.0).astype(BF16)
        prod[u] = jnp.dot(left[u], both, preferred_element_type=F32)
        prod_t[u] = jnp.dot(left_t[u], both_grad, preferred_element_type=F32)
        prod_p[u] = lax.dot_general(left_p[u], both, (((1,), (1,)), ((), ())), preferred_element_type=F32)
        conv = prod[u, :length, :]
        mixed_grad = prod_t[u, :length, :]
        sums = []
        for g in range(per_tile):
            here = slice(g * length, (g + 1) * length)
            if g:
                conv = jnp.where(group_of_lane == g, prod[u, here, :], conv)
                mixed_grad = jnp.where(group_of_lane == g, prod_t[u, here, :], mixed_grad)
            pair = prod_p[u, here, :length] * rev_masks[0] + prod_p[u, here, length:] * rev_masks[1]
            pair = pltpu.roll(pair, 0, 1, stride=1, stride_axis=0)
            sums.append(jnp.sum(pair, axis=0, keepdims=True))
        part[c * slices + i // PAIR, 3 * HALO :, u * LANES : (u + 1) * LANES] = jnp.concatenate(sums, axis=0)
        gated_ref[:, cols] = (qf_ref[:, cols] * conv).astype(BF16)
        products = (
            og_ref[:, cols].astype(F32) * conv, mixed_grad * vf_ref[:, cols], mixed_grad * kf_ref[:, cols],
        )
        for n, product in enumerate(products):
            rounded = product.astype(BF16)
            short_ref[n, :, cols] = rounded
            edge = rounded[:EDGE].astype(F32) * back_masks[fir_len + 1, :EDGE, :]
            head_out[c, n, :, inner] = edge.astype(BF16)

    def long_chunk(c, carry):
        pl.when(has_before)(lambda: mixed_copy(c).wait_recv())
        pl.when(has_after)(lambda: grad_copy(c).wait_recv())

        def pair(i, carry):
            for u in range(PAIR):
                long_tile(c, i * PAIR + u, u)
            return carry

        lax.fori_loop(0, tiles // PAIR, pair, 0)
        pl.when(has_before)(lambda: head_copy(c).start())
        return carry

    lax.fori_loop(0, chunks, long_chunk, 0)
    stores = [
        pltpu.make_async_copy(src, dst, store_sem.at[n])
        for n, (src, dst) in enumerate(
            ((gated_ref, gated_out), (gq_ref, gq_out), (gk_ref, gk_out), (gv_ref, gv_out))
        )
    ]
    stores[0].start()

    def part_copy(target, source):
        return copy(part.at[target], slots.at[source], part_send.at[target], part_recv.at[source], target)

    def backward_chunk(step, carry):
        c = lax.rem(step + 1 + me // slices, chunks)
        pl.when(has_after)(lambda: head_copy(c).wait_recv())

        def pair(i, carry):
            for u in range(PAIR):
                inner = lanes((i * PAIR + u) * LANES)
                start = c * WIDE + (i * PAIR + u) * LANES
                cols = lanes(start)
                for n, (x, out) in enumerate(((q_ref, gq_ref), (k_ref, gk_ref), (v_ref, gv_ref))):
                    e = u * 3 + n
                    ext[e, :length, :] = short_ref[n, :, cols].astype(F32)
                    ext[e, length : length + HALO, :] = head_in[c, n, :, inner].astype(F32)[:HALO]
                    weight = w_ref[:, lanes(n * channels + start)]
                    signal = x[:, cols].astype(F32)
                    total = None
                    sums = []
                    for j in range(fir_len):
                        moved = ext[e, j : j + length, :]
                        if j:
                            moved = moved * fore_masks[j]
                        term = weight[j : j + 1] * moved
                        total = term if total is None else total + term
                        sums.append(jnp.sum(signal * moved, axis=0, keepdims=True))
                    sums.append(jnp.zeros((HALO - fir_len, LANES), F32))
                    out[:, cols] = total.astype(BF16)
                    part[c * slices + i, n * HALO : (n + 1) * HALO, u * LANES : (u + 1) * LANES] = jnp.concatenate(
                        sums, axis=0
                    )
            return carry

        lax.fori_loop(0, slices, pair, 0)
        if summed:
            for s in range(slices):
                target = c * slices + s

                @pl.when(target != me)
                def _():
                    part_copy(target, me).start()

        return carry

    lax.fori_loop(0, chunks, backward_chunk, 0)
    for store in stores[1:]:
        store.start()

    if summed:
        def add(d, total):
            source = lax.rem(me + d, count)
            part_copy(me, source).wait_recv()
            return total + slots[source]

        total = lax.fori_loop(1, count, add, part[me])
        kind = lax.broadcasted_iota(jnp.int32, total.shape, 0)
        sums_ref[me] = total * jnp.where(kind < 3 * HALO, short_scale, med_scale)
        core = lax.rem(me, 2)
        other = me + 1 - 2 * core

        def sum_copy(slot, way, peer):
            return copy(sums_ref.at[slot], sums_ref.at[slot], sum_send.at[way], sum_recv.at[slot], peer)

        chips = count // 2
        for d in range(1, chips):
            sum_copy(me, d, lax.rem(me + 2 * d, count)).start()
        sum_copy(me, 0, other).start()
        for d in range(1, chips):
            slot = lax.rem(me + count - 2 * d, count)
            sum_copy(slot, d, other).wait_recv()
            sum_copy(slot, chips + d, other).start()
        for d in range(chips):
            slot = lax.rem(other + count - 2 * d, count)
            sum_copy(slot, d, other).wait_recv()
        for d in range(1, chips):
            sum_copy(me, d, lax.rem(me + 2 * d, count)).wait_send()
            sum_copy(me, chips + d, other).wait_send()
        sum_copy(me, 0, other).wait_send()

        def drain(d, carry):
            part_copy(lax.rem(me + d, count), me).wait_send()
            return carry

        lax.fori_loop(1, count, drain, 0)
    else:
        sums_ref[...] = part[...]

    @pl.when(has_after)
    def _():
        tail_copy().wait_send()

    def finish(c, carry):
        @pl.when(has_after)
        def _():
            mixed_copy(c).wait_send()

        @pl.when(has_before)
        def _():
            grad_copy(c).wait_send()
            head_copy(c).wait_send()

        return carry

    lax.fori_loop(0, chunks, finish, 0)
    for store in stores:
        store.wait()


def hand_on(*refs):
    for source, target in zip(refs[:4], refs[4:]):
        target[...] = source[...]


def local(query_proj, key_proj, value_proj, out_grad, short_taps, medium_taps, doc_starts, continues):
    length, channels = query_proj.shape
    groups, med_len = medium_taps.shape
    size = channels // groups
    per_tile = LANES // size
    fir_len = short_taps.shape[0]
    count = lax.axis_size("ctx")
    chunks, pieces = channels // WIDE, channels // SLICE
    summed = pieces == count
    tokens = length * count
    short_scale = 1.0 / math.sqrt(tokens)
    med_scale = 1.0 / math.sqrt(tokens * size)
    taps_f = short_taps.astype(F32)
    med_f = medium_taps.astype(F32)
    turned = jnp.roll(jnp.flip(med_f, axis=1), 1, axis=1)
    shape = jax.ShapeDtypeStruct
    half = shape((length, channels), BF16)
    vmem = pl.BlockSpec(memory_space=pltpu.VMEM)
    smem = pl.BlockSpec(memory_space=pltpu.SMEM)
    dma = pltpu.SemaphoreType.DMA
    buffer = pltpu.VMEM
    gated, gq, gk, gv, sums = pl.pallas_call(
        functools.partial(layer, count, summed, short_scale, med_scale),
        in_specs=[smem] * 2 + [vmem] * 7,
        out_specs=[pl.BlockSpec(memory_space=pltpu.HBM)] * 4 + [vmem],
        out_shape=[half] * 4 + [shape((pieces, 4 * HALO, SLICE), F32)],
        scratch_shapes=[buffer((length, channels), BF16)] * 4
        + [buffer((length, channels), F32)] * 3
        + [buffer((length, channels), BF16)] * 2
        + [buffer((3, length, channels), BF16)]
        + [buffer((3, EDGE, channels), BF16)] * 2
        + [buffer((chunks, length, WIDE), BF16)] * 4
        + [buffer((chunks, 3, EDGE, WIDE), BF16)] * 2
        + [buffer((pieces, 4 * HALO, SLICE), F32)] * 2
        + [
            buffer((fir_len + 2, length, LANES), F32),
            buffer((fir_len, length, LANES), F32),
            buffer((4, length, length), BF16),
            buffer((2, length, length), F32),
            buffer((length, length), BF16),
            buffer((3 * PAIR, length + HALO, LANES), F32),
            buffer((PAIR, per_tile * length, 2 * length), BF16),
            buffer((PAIR, per_tile * length, 2 * length), BF16),
            buffer((PAIR, per_tile * length, LANES), BF16),
            buffer((PAIR, per_tile * length, LANES), F32),
            buffer((PAIR, per_tile * length, LANES), F32),
            buffer((PAIR, per_tile * length, 2 * length), F32),
        ]
        + [dma(())] * 2
        + [dma((chunks,))] * 6
        + [dma((count,))] * 4
        + [dma((4,))],
        compiler_params=pltpu.CompilerParams(
            vmem_limit_bytes=VMEM_BYTES, collective_id=0, has_side_effects=True
        ),
    )(doc_starts, continues, query_proj, key_proj, value_proj, out_grad, taps_f, med_f, turned)
    block = pl.BlockSpec((length, channels // 4), lambda i: (0, i))
    gated, gq, gk, gv = pl.pallas_call(
        hand_on,
        grid=(4,),
        in_specs=[block] * 4,
        out_specs=[block] * 4,
        out_shape=[half] * 4,
        compiler_params=pltpu.CompilerParams(vmem_limit_bytes=VMEM_BYTES),
    )(gated, gq, gk, gv)
    if not summed:
        sums = lax.psum(sums, "ctx")
        sums = jnp.concatenate([sums[:, : 3 * HALO] * short_scale, sums[:, 3 * HALO :] * med_scale], axis=1)
    short = sums[:, : 3 * HALO].reshape(pieces, 3, HALO, SLICE)[:, :, :fir_len]
    grad_short = short.transpose(2, 1, 0, 3).reshape(fir_len, 3 * channels)
    medium = sums[:, 3 * HALO :].reshape(pieces, HALO, SLICE // LANES, LANES).transpose(0, 2, 1, 3)
    grad_medium = jnp.flip(medium.reshape(groups, med_len), axis=1)
    return gated, gq, gk, gv, grad_short, grad_medium


def solution(mesh):
    tokens = P(("grp", "ctx"), None)
    in_specs = (tokens,) * 4 + (P(), P(), tokens, P(("grp", "ctx")))
    out_specs = (tokens,) * 4 + (P("grp", None), P("grp", None))
    return jax.shard_map(local, mesh=mesh, in_specs=in_specs, out_specs=out_specs, check_vma=False)
```
